256 devices in a mesh: ctx: 64 (over z, x_hi, y), chan: 4 (over x_lo, core).
Axes of the slice: x: 4 (x_hi: 2, x_lo: 2; x = x_hi * 2 + x_lo), y: 4, z: 8, core: 2. Of those that a mesh axis runs over, the one named last changes fastest.
Arguments:
- projected: bfloat16 [16384, 3, 4096], P('ctx', None, 'chan'), may hold values from -6 to 6
- short_taps: float32 [3, 3, 4096], P(None, None, 'chan'), may hold values from -3 to 3
- decay_rates: float32 [4096, 16], P('chan'), may hold values from 0 to 0.034, as said below
- residues: float32 [4096, 16], P('chan')
- out_weight: bfloat16 [4096, 4096], P(None, 'chan'), may hold values from -0.09375 to 0.09375
Outputs:
- mixed: bfloat16 [16384, 4096], P('ctx', 'chan')
The draws below stay inside these ranges and needn't reach their ends.
Inputs may be any that keep to these rules, and one draw needn't show every extreme that they name: `decay_rates`: every decay rate is positive.
All inputs are finite; a program needn't handle non-finite values.
Results may differ from the reference program's by a relative error of at most 0.0049.
Values may be sent and summed in bfloat16 or wider, within the bound.
No kernel may reach another device: no remote copies, remote signals or barrier semaphores. Data moves between devices by JAX's collectives and lax.ppermute only.
A program may use at most 128 MiB of HBM per device.

```python
import jax
import jax.numpy as jnp
from jax import lax

D = 4096
C = 4096
M = 16
TAPS = 3
TOKENS = 16384


def mode_rates(key, lowest, highest):
    rate_key = jax.random.fold_in(key, 11)
    fraction = jax.random.uniform(rate_key, (C, M), jnp.float32)
    return jnp.exp(jnp.log(lowest) + fraction * (jnp.log(highest) - jnp.log(lowest)))


def draw_decay_rates(key, part):
    rates = mode_rates(key, 0.3 / TOKENS, 1.0 / 30.0)
    return rates


def draw_residues(key, part):
    rates = mode_rates(key, 0.3 / TOKENS, 1.0 / 30.0)
    own_key = jax.random.fold_in(key, 23)
    return jax.random.normal(own_key, (C, M), jnp.float32) * jnp.sqrt(2.0 * rates / M)


def block_scale(rng, dims, shards, smallest, high):
    loudness, own = 1.0, jax.random.fold_in(rng, 6)
    for dim, shards_of in shards:
        heights = jnp.exp(jax.random.uniform(jax.random.fold_in(own, dim), (shards_of,), jnp.float32, smallest / len(shards), high / len(shards)))
        loudness = loudness * jnp.repeat(heights, dims[dim] // shards_of).reshape([-1 if axis == dim else 1 for axis in range(len(dims))])
    return loudness


def scatter_about(rng, extent, deviation, limit, shards=(), kind=jnp.bfloat16):
    values = deviation * jax.random.normal(rng, extent, jnp.float32)
    if shards:
        values = values * block_scale(rng, extent, shards, -0.22, 0.18)
    return jnp.clip(values, -limit, limit).astype(kind)


def setup_inputs(seed: int = 0) -> dict:
    splits = jax.random.split(jax.random.key(seed), 6)
    return {
        "projected": scatter_about(splits[0], (TOKENS, 3, C), 1.0, 6.0, ((0, 64), (2, 4))),
        "short_taps": scatter_about(splits[1], (3, TAPS, C), 0.6, 3.0, ((2, 4),), jnp.float32),
        "decay_rates": draw_decay_rates(jax.random.fold_in(splits[5], 71), 0),
        "residues": draw_residues(jax.random.fold_in(splits[5], 71), 0),
        "out_weight": scatter_about(splits[4], (C, D), C ** -0.5, 0.09375, ((1, 4),)),
    }


def short_filter(projected, short_taps):
    values = projected.astype(jnp.float32)
    length = values.shape[0]
    result = short_taps[:, 0, :][None] * values
    for offset in range(1, TAPS):
        delayed = jnp.concatenate([jnp.zeros((offset,) + values.shape[1:], values.dtype), values[: length - offset]], axis=0)
        result = result + short_taps[:, offset, :][None] * delayed
    return result


def modal_filter(decay_rates, residues, length):
    moments = jnp.arange(length).astype(decay_rates.dtype)
    result = jnp.zeros((decay_rates.shape[0], length), decay_rates.dtype)
    for column in range(decay_rates.shape[1]):
        result = result + residues[:, column, None] * jnp.exp(-decay_rates[:, column, None] * moments[None, :])
    return result


def group_conv(operands):
    signal, rates_group, residue_group = operands
    length = signal.shape[1]
    kernel = modal_filter(rates_group, residue_group, length)
    spectrum = jnp.fft.rfft(signal, 2 * length, axis=1) * jnp.fft.rfft(kernel, 2 * length, axis=1)
    return jnp.fft.irfft(spectrum, 2 * length, axis=1)[:, :length]


def reference(projected, short_taps, decay_rates, residues, out_weight):
    features = short_filter(projected, short_taps)
    mixed_input = features[:, 1, :] * features[:, 2, :]
    channels = mixed_input.shape[1]
    group_size = min(channels, 32)
    num_groups = channels // group_size
    signal = mixed_input.T.reshape(num_groups, group_size, -1)
    convolved = lax.map(group_conv, (signal, decay_rates.reshape(num_groups, group_size, -1), residues.reshape(num_groups, group_size, -1)))
    long_out = convolved.reshape(channels, -1).T
    gated = (features[:, 0, :] * long_out).astype(jnp.bfloat16)
    return jnp.dot(gated, out_weight, preferred_element_type=jnp.float32).astype(jnp.bfloat16)
```

```python
import functools

import jax
import jax.numpy as jnp
from jax import lax
from jax.experimental import pallas as pl
from jax.experimental.pallas import tpu as pltpu
from jax.sharding import PartitionSpec as P

TAPS = 3
LANES = 128
ROWS = 8
CHUNKS = 4
VMEM = pl.BlockSpec(memory_space=pltpu.VMEM)


def params(mib):
    return pltpu.CompilerParams(vmem_limit_bytes=mib * 1024 * 1024)


def short_filter(x_ref, first, taps, lanes):
    block = x_ref.shape[0] - ROWS
    out = taps[0:1, lanes] * x_ref[pl.ds(ROWS, block), :]
    out = out + taps[1:2, lanes] * x_ref[pl.ds(ROWS - 1, block), :]
    return out + taps[2:3, lanes] * x_ref[pl.ds(ROWS - 2, block), :]


def end_state_kernel(p_ref, taps_ref, rates_ref, out_ref, k_ref, v_ref, u_ref):
    block, channels = p_ref.shape[1:]
    k_ref[pl.ds(0, ROWS), :] = jnp.zeros((ROWS, LANES), jnp.float32)
    v_ref[pl.ds(0, ROWS), :] = jnp.zeros((ROWS, LANES), jnp.float32)
    modes = rates_ref.shape[0]
    row = lax.broadcasted_iota(jnp.int32, (ROWS, LANES), 0).astype(jnp.float32)

    def lane_block(c, carry):
        lanes = pl.ds(pl.multiple_of(c * LANES, LANES), LANES)
        k_ref[pl.ds(ROWS, block), :] = p_ref[1, :, lanes].astype(jnp.float32)
        v_ref[pl.ds(ROWS, block), :] = p_ref[2, :, lanes].astype(jnp.float32)
        u = short_filter(k_ref, 0, taps_ref.at[1], lanes) * short_filter(v_ref, 0, taps_ref.at[2], lanes)
        u_ref[...] = u
        u_ref[pl.ds(0, ROWS), :] = jnp.where(row < TAPS - 1, 0.0, u[:ROWS])
        rates = [jnp.broadcast_to(rates_ref[m : m + 1, lanes], (ROWS, LANES)) for m in range(modes)]
        steps = [jnp.exp(-float(ROWS) * r) for r in rates]
        state = [u_ref[pl.ds(0, ROWS), :]] * modes
        for j in range(1, block // ROWS):
            now = u_ref[pl.ds(j * ROWS, ROWS), :]
            state = [a * s + now for a, s in zip(steps, state)]
        for m in range(modes):
            weighted = state[m] * jnp.exp(rates[m] * (row - (ROWS - 1.0)))
            out_ref[m : m + 1, lanes] = jnp.sum(weighted, axis=0, keepdims=True)
        return carry

    lax.fori_loop(0, channels // LANES, lane_block, 0)


def end_state(p, taps, rates):
    block, channels = p.shape[1:]
    return pl.pallas_call(
        end_state_kernel,
        out_shape=jax.ShapeDtypeStruct(rates.shape, jnp.float32),
        in_specs=[VMEM] * 3,
        out_specs=VMEM,
        scratch_shapes=[
            pltpu.VMEM((ROWS + block, LANES), jnp.float32),
            pltpu.VMEM((ROWS + block, LANES), jnp.float32),
            pltpu.VMEM((block, LANES), jnp.float32),
        ],
        compiler_params=params(16),
        name="end_state",
    )(p, taps, rates)


def local_kernel(p_ref, prev_ref, taps_ref, rates_ref, res_ref, y_ref, q_out_ref, x_ref, u_ref, a_ref, r_ref):
    block, channels = p_ref.shape[1:]
    modes = rates_ref.shape[0]
    groups, cblocks = block // ROWS, channels // LANES
    for c in range(cblocks):
        lanes = pl.ds(c * LANES, LANES)
        feats = []
        for i in range(3):
            before = prev_ref[i, :, lanes].astype(jnp.float32)
            x_ref[pl.ds(ROWS - 2, 2), :] = before
            x_ref[pl.ds(ROWS, block), :] = p_ref[i, :, lanes].astype(jnp.float32)
            feats.append(short_filter(x_ref, 0, taps_ref.at[i], lanes))
        u = feats[1] * feats[2]
        for j in range(groups):
            rows = pl.ds(j * ROWS * cblocks + c * ROWS, ROWS)
            u_ref[rows, :] = u[j * ROWS : (j + 1) * ROWS]
            q_out_ref[rows, :] = feats[0][j * ROWS : (j + 1) * ROWS]
        for m in range(0, modes, ROWS):
            rows = pl.ds(m * cblocks + c, ROWS, stride=cblocks)
            a_ref[rows, :] = jnp.exp(-rates_ref[m : m + ROWS, lanes])
            r_ref[rows, :] = res_ref[m : m + ROWS, lanes]

    def group(j, state):
        state = list(state)
        for i in range(ROWS):
            at = pl.ds(j * ROWS * cblocks + i, cblocks, stride=ROWS)
            now = u_ref[at, :]
            total = [None] * 4
            for m in range(modes):
                a = a_ref[pl.ds(m * cblocks, cblocks), :]
                r = r_ref[pl.ds(m * cblocks, cblocks), :]
                state[m] = a * state[m] + now
                term = r * state[m]
                total[m % 4] = term if total[m % 4] is None else total[m % 4] + term
            y_ref[at, :] = (total[0] + total[1]) + (total[2] + total[3])
        return tuple(state)

    zero = jnp.zeros((cblocks, LANES), jnp.float32)
    lax.fori_loop(0, groups, group, (zero,) * modes)


def local_part(p, prev, taps, rates, residues):
    block, channels = p.shape[1:]
    modes = rates.shape[0]
    cblocks = channels // LANES
    tiled = jax.ShapeDtypeStruct((block * cblocks, LANES), jnp.float32)
    return pl.pallas_call(
        local_kernel,
        out_shape=(tiled, tiled),
        in_specs=[VMEM] * 5,
        out_specs=(VMEM, VMEM),
        scratch_shapes=[
            pltpu.VMEM((ROWS + block, LANES), jnp.float32),
            pltpu.VMEM((block * cblocks, LANES), jnp.float32),
            pltpu.VMEM((modes * cblocks, LANES), jnp.float32),
            pltpu.VMEM((modes * cblocks, LANES), jnp.float32),
        ],
        compiler_params=params(16),
        cost_estimate=pl.CostEstimate(flops=4 * modes * block * channels, bytes_accessed=6 * block * channels, transcendentals=0),
        name="local_part",
    )(p, prev, taps, rates, residues)


def gate_kernel(y_ref, q_ref, state_ref, rates_ref, res_ref, out_ref):
    groups, cblocks = y_ref.shape[:2]
    modes = rates_ref.shape[0]
    row = lax.broadcasted_iota(jnp.int32, (ROWS, LANES), 0).astype(jnp.float32)
    for c in range(cblocks):
        lanes = pl.ds(c * LANES, LANES)
        terms, steps = [], []
        for m in range(modes):
            rate = jnp.broadcast_to(rates_ref[m : m + 1, lanes], (ROWS, LANES))
            scale = res_ref[m : m + 1, lanes] * state_ref[m : m + 1, lanes]
            terms.append(jnp.exp(-rate * (row + 1.0)) * scale)
            steps.append(jnp.exp(-float(ROWS) * rate))

        def pair(jj, terms):
            terms = list(terms)
            halves = []
            for half in range(2):
                total = [y_ref[2 * jj + half, c], None, None, None]
                for m in range(modes):
                    total[m % 4] = terms[m] if total[m % 4] is None else total[m % 4] + terms[m]
                    terms[m] = terms[m] * steps[m]
                halves.append(q_ref[2 * jj + half, c] * ((total[0] + total[1]) + (total[2] + total[3])))
            both = jnp.concatenate(halves, axis=0).astype(out_ref.dtype)
            out_ref[pl.ds(pl.multiple_of(jj * 2 * ROWS, 2 * ROWS), 2 * ROWS), lanes] = both
            return tuple(terms)

        lax.fori_loop(0, groups // 2, pair, tuple(terms), unroll=4)


def gate(part, parts, y, q, state, rates, residues):
    modes, channels = rates.shape
    cblocks = channels // LANES
    block = y.shape[0] // cblocks
    y, q = (value.reshape(block // ROWS, cblocks, ROWS, LANES) for value in (y, q))
    own = cblocks // parts
    rows = pl.BlockSpec((block // ROWS, own, ROWS, LANES), lambda g: (0, part, 0, 0))
    table = pl.BlockSpec((modes, own * LANES), lambda g: (0, part))
    return pl.pallas_call(
        gate_kernel,
        grid=(1,),
        out_shape=jax.ShapeDtypeStruct((block, own * LANES), jnp.bfloat16),
        in_specs=[rows, rows, table, table, table],
        out_specs=pl.BlockSpec((block, own * LANES), lambda g: (0, 0)),
        compiler_params=params(16),
        cost_estimate=pl.CostEstimate(flops=2 * modes * block * own * LANES, bytes_accessed=10 * block * own * LANES, transcendentals=0),
        name="gate",
    )(y, q, state, rates, residues)


def project_kernel(last, order_ref, acc_ref, p0, p1, p2, p3, w_ref, out_ref, total_ref):
    step = pl.program_id(0)

    @pl.when(step == 0)
    def _():
        total_ref[...] = acc_ref[...] if acc_ref is not None else jnp.zeros_like(total_ref)

    for number, piece in enumerate((p0, p1, p2, p3)):

        @pl.when(step == number)
        def _():
            total_ref[...] += jnp.dot(piece[...], w_ref[...], preferred_element_type=jnp.float32)

    @pl.when(step == 3)
    def _():
        out_ref[...] = total_ref[...].astype(out_ref.dtype)


def project(part, parts, order, acc, pieces, weight):
    block, depth = pieces[0].shape
    features = weight.shape[1]
    last = part == parts - 1
    whole = lambda shape: pl.BlockSpec(shape, lambda g, order: (0, 0))
    kernel = functools.partial(project_kernel, last)
    if acc is None:
        kernel = lambda order_ref, *refs: project_kernel(last, order_ref, None, *refs)
    grid_spec = pltpu.PrefetchScalarGridSpec(
        num_scalar_prefetch=1,
        grid=(4,),
        in_specs=([] if acc is None else [whole((block, features))])
        + [whole((block, depth))] * 4
        + [pl.BlockSpec((depth, features), lambda g, order: (order[g] * parts + part, 0))],
        out_specs=whole((block, features)),
        scratch_shapes=[pltpu.VMEM((block, features), jnp.float32)],
    )
    return pl.pallas_call(
        kernel,
        grid_spec=grid_spec,
        out_shape=jax.ShapeDtypeStruct((block, features), jnp.bfloat16 if last else jnp.float32),
        compiler_params=params(16),
        cost_estimate=pl.CostEstimate(flops=8 * block * depth * features, bytes_accessed=8 * depth * features, transcendentals=0),
        name="project",
    )(order, *(() if acc is None else (acc,)), *pieces, weight)


def partners(count):
    levels, size = [], 1
    while size < count:
        if size in (2, 32):
            ring = 4 if size == 2 else 8
            unit = size * 2 // ring
            flip = lambda i: (i // (unit * ring)) * unit * ring + (ring - 1 - i // unit % ring) * unit + i % unit
        else:
            flip = lambda i: i ^ size
        levels.append((size, [flip(i) for i in range(count)]))
        size *= 2
    return levels


def states_before(end, rates, block):
    count = lax.axis_size("ctx")
    position = lax.axis_index("ctx")
    total, before = end, jnp.zeros_like(end)
    for size, partner in partners(count):
        other = lax.ppermute(total, "ctx", list(enumerate(partner)))
        later = (position // size) % 2 == 1
        offset = (position % size).astype(jnp.float32)
        decay = jnp.exp(-rates * (block * offset))
        before = before + jnp.where(later, other * decay, 0.0)
        whole = jnp.exp(-rates * float(block * size))
        total = jnp.where(later, other * whole + total, total * whole + other)
    return before


def per_device(projected, short_taps, decay_rates, residues, out_weight):
    block = projected.shape[0]
    count = lax.axis_size("ctx")
    p = projected.transpose(1, 0, 2)
    rates, res = decay_rates.T, residues.T

    prev = lax.ppermute(p[:, block - (TAPS - 1) :], "ctx", [(i, i + 1) for i in range(count - 1)])
    end = end_state(p, short_taps, rates)
    head = jnp.concatenate([prev, p[:, : TAPS - 1]], axis=1).astype(jnp.float32)
    feats = sum(short_taps[:, j, None] * head[:, TAPS - 1 - j : 2 * (TAPS - 1) - j] for j in range(TAPS))
    first = feats[1] * feats[2]
    for t in range(TAPS - 1):
        end = end + jnp.exp(-rates * float(block - 1 - t)) * first[t][None]

    before = states_before(end, rates, block)
    y, q = local_part(p, prev, short_taps, rates, res)

    own = lax.axis_index("chan")
    order = jnp.stack([own, own ^ 2, own ^ 1, own ^ 3]).astype(jnp.int32)
    over_x = [(i, i ^ 2) for i in range(4)]
    over_core = [(i, i ^ 1) for i in range(4)]
    acc = None
    for part in range(CHUNKS):
        mine = gate(part, CHUNKS, y, q, before, rates, res)
        across = lax.ppermute(mine, "chan", over_x)
        beside = lax.ppermute(mine, "chan", over_core)
        far = lax.ppermute(across, "chan", over_core)
        acc = project(part, CHUNKS, order, acc, (mine, across, beside, far), out_weight)
    return acc


def solution(mesh):
    in_specs = (
        P("ctx", None, "chan"),
        P(None, None, "chan"),
        P("chan", None),
        P("chan", None),
        P(None, "chan"),
    )
    return jax.shard_map(
        per_device, mesh=mesh, in_specs=in_specs, out_specs=P("ctx", "chan"), check_vma=False
    )
```

```python
import functools

import jax
import jax.numpy as jnp
from jax import lax
from jax.experimental import pallas as pl
from jax.experimental.pallas import tpu as pltpu
from jax.sharding import PartitionSpec as P

TAPS = 3
LANES = 128
ROWS = 8
INPUT_COST = 8 * 10**9
PARTS = (512, 512)
LOCAL_AT = 2
LOCAL_LIMIT = 50
INPUT_LIMIT = 52
LOAD_LIMIT = 38
HOLD = 9
VMEM = pl.BlockSpec(memory_space=pltpu.VMEM)
HBM = pl.BlockSpec(memory_space=pltpu.HBM)
SMEM = pl.BlockSpec(memory_space=pltpu.SMEM)


def params(mib):
    return pltpu.CompilerParams(vmem_limit_bytes=mib * 1024 * 1024)


def cost(flops, moved):
    return pl.CostEstimate(flops=flops, bytes_accessed=moved, transcendentals=0)


def short_filter(x_ref, tokens, taps, lanes):
    out = taps[0:1, lanes] * x_ref[pl.ds(ROWS, tokens), :]
    out = out + taps[1:2, lanes] * x_ref[pl.ds(ROWS - 1, tokens), :]
    return out + taps[2:3, lanes] * x_ref[pl.ds(ROWS - 2, tokens), :]


def input_kernel(p_hbm, taps_ref, u_ref, head_ref, taps_out, kv_ref, k_pad, v_pad, sems):
    block, channels = kv_ref.shape[1:]
    cblocks = channels // LANES
    copies = [pltpu.make_async_copy(p_hbm.at[1 + i], kv_ref.at[i], sems.at[i]) for i in range(2)]
    for copy in copies:
        copy.start()
    taps_out[...] = taps_ref[...]
    k_pad[pl.ds(0, ROWS), :] = jnp.zeros((ROWS, LANES), jnp.float32)
    v_pad[pl.ds(0, ROWS), :] = jnp.zeros((ROWS, LANES), jnp.float32)
    row = lax.broadcasted_iota(jnp.int32, (ROWS, LANES), 0)
    for copy in copies:
        copy.wait()
    for c in range(cblocks):
        lanes = pl.ds(c * LANES, LANES)
        k_pad[pl.ds(ROWS, block), :] = kv_ref[0, :, lanes].astype(jnp.float32)
        v_pad[pl.ds(ROWS, block), :] = kv_ref[1, :, lanes].astype(jnp.float32)
        head_ref[0, :, lanes] = k_pad[pl.ds(ROWS, TAPS - 1), :]
        head_ref[1, :, lanes] = v_pad[pl.ds(ROWS, TAPS - 1), :]
        u = short_filter(k_pad, block, taps_ref.at[1], lanes) * short_filter(v_pad, block, taps_ref.at[2], lanes)
        for j in range(block // ROWS):
            part = u[j * ROWS : (j + 1) * ROWS]
            u_ref[pl.ds((j * cblocks + c) * ROWS, ROWS), :] = part if j else jnp.where(row < TAPS - 1, 0.0, part)


def conv_input(p, taps):
    block, channels = p.shape[1:]
    padded = pltpu.VMEM((ROWS + block, LANES), jnp.float32)
    return pl.pallas_call(
        input_kernel,
        out_shape=(
            jax.ShapeDtypeStruct((block * channels // LANES, LANES), jnp.float32),
            jax.ShapeDtypeStruct((2, TAPS - 1, channels), jnp.float32),
            jax.ShapeDtypeStruct(taps.shape, taps.dtype),
        ),
        in_specs=[HBM, VMEM],
        out_specs=(VMEM,) * 3,
        scratch_shapes=[pltpu.VMEM((2, block, channels), p.dtype), padded, padded, pltpu.SemaphoreType.DMA((2,))],
        compiler_params=params(INPUT_LIMIT),
        cost_estimate=cost(INPUT_COST, 6 * block * channels),
        name="conv_input",
    )(p, taps)


def end_state_kernel(u_ref, rates_ref, res_ref, out_ref, tables_ref):
    modes, channels = rates_ref.shape
    cblocks = channels // LANES
    groups = u_ref.shape[0] // (cblocks * ROWS)
    row = lax.broadcasted_iota(jnp.int32, (ROWS, LANES), 0).astype(jnp.float32)
    tables_ref[0] = rates_ref[...]
    tables_ref[1] = res_ref[...]

    def lane_block(c, carry):
        lanes = pl.ds(pl.multiple_of(c * LANES, LANES), LANES)
        rates = [jnp.broadcast_to(rates_ref[m : m + 1, lanes], (ROWS, LANES)) for m in range(modes)]
        steps = [jnp.exp(-float(ROWS) * r) for r in rates]
        state = [u_ref[pl.ds(pl.multiple_of(c * ROWS, ROWS), ROWS), :]] * modes
        for j in range(1, groups):
            now = u_ref[pl.ds(pl.multiple_of((j * cblocks + c) * ROWS, ROWS), ROWS), :]
            state = [a * s + now for a, s in zip(steps, state)]
        for m in range(modes):
            weighted = state[m] * jnp.exp(rates[m] * (row - (ROWS - 1.0)))
            out_ref[m : m + 1, lanes] = jnp.sum(weighted, axis=0, keepdims=True)
        return carry

    lax.fori_loop(0, cblocks, lane_block, 0)


def end_state(u, rates, residues):
    return pl.pallas_call(
        end_state_kernel,
        out_shape=(
            jax.ShapeDtypeStruct(rates.shape, jnp.float32),
            jax.ShapeDtypeStruct((2, *rates.shape), jnp.float32),
        ),
        in_specs=[VMEM] * 3,
        out_specs=(VMEM,) * 2,
        compiler_params=params(8),
        cost_estimate=cost(2 * rates.shape[0] * u.size, 4 * u.size),
        name="end_state",
    )(u, rates, residues)


def local_kernel(p_hbm, prev_ref, taps_ref, tables_ref, in_ref, first_ref, y_ref, f_ref, q_ref, x_ref, u_ref, a_ref, r_ref, q_sem):
    block, channels = q_ref.shape
    modes = tables_ref.shape[1]
    cblocks = channels // LANES
    groups = block // ROWS
    q_copy = pltpu.make_async_copy(p_hbm.at[0], q_ref, q_sem)
    q_copy.start()
    u_ref[...] = in_ref[...]
    for c in range(cblocks):
        lanes = pl.ds(c * LANES, LANES)
        for t in range(TAPS - 1):
            u_ref[pl.ds(c * ROWS + t, 1), :] = first_ref[t : t + 1, lanes]
        for m in range(0, modes, ROWS):
            rows = pl.ds(m * cblocks + c, ROWS, stride=cblocks)
            a_ref[rows, :] = jnp.exp(-tables_ref[0, m : m + ROWS, lanes])
            r_ref[rows, :] = tables_ref[1, m : m + ROWS, lanes]

    def group(j, state):
        state = list(state)
        for i in range(ROWS):
            at = pl.ds(j * ROWS * cblocks + i, cblocks, stride=ROWS)
            now = u_ref[at, :]
            total = [None] * 4
            for m in range(modes):
                a = a_ref[pl.ds(m * cblocks, cblocks), :]
                r = r_ref[pl.ds(m * cblocks, cblocks), :]
                state[m] = a * state[m] + now
                term = r * state[m]
                total[m % 4] = term if total[m % 4] is None else total[m % 4] + term
            y_ref[at, :] = (total[0] + total[1]) + (total[2] + total[3])
        return tuple(state)

    lax.fori_loop(0, groups, group, (jnp.zeros((cblocks, LANES), jnp.float32),) * modes)
    q_copy.wait()
    for c in range(cblocks):
        lanes = pl.ds(c * LANES, LANES)
        x_ref[pl.ds(ROWS - 2, 2), :] = prev_ref[0, :, lanes].astype(jnp.float32)
        x_ref[pl.ds(ROWS, block), :] = q_ref[:, lanes].astype(jnp.float32)
        feature = short_filter(x_ref, block, taps_ref.at[0], lanes)
        for j in range(groups):
            f_ref[pl.ds((j * cblocks + c) * ROWS, ROWS), :] = feature[j * ROWS : (j + 1) * ROWS]


def local_part(p, prev, taps, tables, u, first):
    block, channels = p.shape[1:]
    modes = tables.shape[1]
    cblocks = channels // LANES
    table = pltpu.VMEM((modes * cblocks, LANES), jnp.float32)
    tiled = jax.ShapeDtypeStruct((block * cblocks, LANES), jnp.float32)
    return pl.pallas_call(
        local_kernel,
        out_shape=(tiled, tiled),
        in_specs=[HBM] + [VMEM] * 5,
        out_specs=(VMEM, VMEM),
        scratch_shapes=[
            pltpu.VMEM((block, channels), p.dtype),
            pltpu.VMEM((ROWS + block, LANES), jnp.float32),
            pltpu.VMEM((block * cblocks, LANES), jnp.float32),
            table,
            table,
            pltpu.SemaphoreType.DMA,
        ],
        compiler_params=params(LOCAL_LIMIT),
        cost_estimate=cost(4 * modes * block * channels, 6 * block * channels),
        name="local_part",
    )(p, prev, taps, tables, u, first)


def gate_kernel(first, y_ref, f_ref, state_ref, tables_ref, out_ref):
    modes = tables_ref.shape[1]
    cblocks = tables_ref.shape[2] // LANES
    row = lax.broadcasted_iota(jnp.int32, (ROWS, LANES), 0).astype(jnp.float32)
    for c in range(out_ref.shape[1] // LANES):
        block = first // LANES + c
        lanes = pl.ds(first + c * LANES, LANES)
        terms, steps = [], []
        for m in range(modes):
            rate = jnp.broadcast_to(tables_ref[0, m : m + 1, lanes], (ROWS, LANES))
            scale = tables_ref[1, m : m + 1, lanes] * state_ref[m : m + 1, lanes]
            terms.append(jnp.exp(-rate * (row + 1.0)) * scale)
            steps.append(jnp.exp(-float(ROWS) * rate))

        def pair(jj, terms):
            terms = list(terms)
            both = []
            for half in range(2):
                at = pl.ds(pl.multiple_of(((2 * jj + half) * cblocks + block) * ROWS, ROWS), ROWS)
                total = [y_ref[at, :], None, None, None]
                for m in range(modes):
                    total[m % 4] = terms[m] if total[m % 4] is None else total[m % 4] + terms[m]
                    terms[m] = terms[m] * steps[m]
                both.append(f_ref[at, :] * ((total[0] + total[1]) + (total[2] + total[3])))
            rows = pl.ds(pl.multiple_of(jj * 2 * ROWS, 2 * ROWS), 2 * ROWS)
            out_ref[rows, pl.ds(c * LANES, LANES)] = jnp.concatenate(both, axis=0).astype(out_ref.dtype)
            return tuple(terms)

        lax.fori_loop(0, out_ref.shape[0] // (2 * ROWS), pair, tuple(terms), unroll=4)


def gate(first, last, y, f, state, tables):
    modes, channels = tables.shape[1:]
    block = y.shape[0] * LANES // channels
    size = block * (last - first)
    return pl.pallas_call(
        functools.partial(gate_kernel, first),
        out_shape=jax.ShapeDtypeStruct((block, last - first), jnp.bfloat16),
        in_specs=[VMEM] * 4,
        out_specs=VMEM,
        compiler_params=params(4),
        cost_estimate=cost(2 * modes * size, 6 * size),
        name="gate",
    )(y, f, state, tables)


def load_kernel(order_ref, w_hbm, *refs):
    rows_refs, sems = refs[:4], refs[4]
    depth = w_hbm.shape[0] // 4
    copies = []
    for number, rows_ref in enumerate(rows_refs):
        rows = pl.ds(pl.multiple_of(order_ref[number] * depth, depth), depth)
        copies.append(pltpu.make_async_copy(w_hbm.at[rows, :], rows_ref, sems.at[number]))
        copies[-1].start()
    for copy in copies:
        copy.wait()


def load_rows(order, weight):
    depth, features = weight.shape[0] // 4, weight.shape[1]
    return pl.pallas_call(
        load_kernel,
        out_shape=[jax.ShapeDtypeStruct((depth, features), weight.dtype)] * 4,
        in_specs=[SMEM, HBM],
        out_specs=[VMEM] * 4,
        scratch_shapes=[pltpu.SemaphoreType.DMA((4,))],
        compiler_params=params(LOAD_LIMIT),
        cost_estimate=cost(0, 2 * weight.size),
        name="load_rows",
    )(order, weight)


def project_kernel(first, has_acc, *refs):
    count = 4
    pieces, loaded, out_ref = refs[:count], refs[count : 2 * count], refs[-1]
    total = refs[2 * count][...] if has_acc else None
    for piece, rows_ref in zip(pieces, loaded):
        rows = rows_ref[pl.ds(first, piece.shape[1]), :]
        term = jnp.dot(piece[...], rows, preferred_element_type=jnp.float32)
        total = term if total is None else total + term
    out_ref[...] = total.astype(out_ref.dtype)


def project(pieces, loaded, first, acc, kind):
    block, features = pieces[0].shape[0], loaded[0].shape[1]
    extra = [] if acc is None else [acc]
    return pl.pallas_call(
        functools.partial(project_kernel, first, len(extra)),
        out_shape=jax.ShapeDtypeStruct((block, features), kind),
        in_specs=[VMEM] * (len(pieces) + len(loaded) + len(extra)),
        out_specs=VMEM,
        compiler_params=params(8),
        cost_estimate=cost(0, 1024),
        name="project",
    )(*pieces, *loaded, *extra)


def partners(count):
    levels, size = [], 1
    while size < count:
        if size in (2, 32):
            ring = 4 if size == 2 else 8
            unit = size * 2 // ring
            flip = lambda i: (i // (unit * ring)) * unit * ring + (ring - 1 - i // unit % ring) * unit + i % unit
        else:
            flip = lambda i: i ^ size
        levels.append((size, [flip(i) for i in range(count)]))
        size *= 2
    return levels


def tied(value, *others):
    return lax.optimization_barrier((value, *others))[0]


def per_device(projected, short_taps, decay_rates, residues, out_weight):
    block, _, channels = projected.shape
    count = lax.axis_size("ctx")
    position = lax.axis_index("ctx")
    own = lax.axis_index("chan")
    order = jnp.stack([own, own ^ 1, own ^ 2, own ^ 3]).astype(jnp.int32)
    over_x = lambda value: lax.ppermute(value, "chan", [(i, i ^ 2) for i in range(4)])
    over_core = lambda value: lax.ppermute(value, "chan", [(i, i ^ 1) for i in range(4)])

    p = projected.transpose(1, 0, 2)
    prev = lax.ppermute(p[:, block - (TAPS - 1) :], "ctx", [(i, i + 1) for i in range(count - 1)])
    u, head, taps = conv_input(p, short_taps)
    total, tables = end_state(u, decay_rates.T, residues.T)
    rates = tables[0]
    head = jnp.concatenate([prev[1:].astype(jnp.float32), head], axis=1)
    feats = sum(taps[1:, j, None] * head[:, TAPS - 1 - j : 2 * (TAPS - 1) - j] for j in range(TAPS))
    first = feats[0] * feats[1]
    for t in range(TAPS - 1):
        total = total + jnp.exp(-rates * float(block - 1 - t)) * first[t][None]

    before = jnp.zeros_like(total)
    due = ()
    for level, (size, partner) in enumerate(partners(count)):
        total, before, *_ = lax.optimization_barrier((total, before, *due))
        due = ()
        other = lax.ppermute(total, "ctx", list(enumerate(partner)))
        if level == LOCAL_AT:
            y, f = local_part(p, prev, taps, tables, u, tied(first, total))
            due = (y,)
        later = (position // size) % 2 == 1
        offset = (position % size).astype(jnp.float32)
        decay = jnp.exp(-rates * (block * offset))
        before = before + jnp.where(later, other * decay, 0.0)
        whole = jnp.exp(-rates * float(block * size))
        total = jnp.where(later, other * whole + total, total * whole + other)

    acc, start, loaded, accs = None, 0, None, []
    for number, width in enumerate(PARTS):
        mine = gate(start, start + width, y, f, before, tables)
        if loaded is None:
            loaded = load_rows(tied(order, mine), out_weight)
        across, beside = over_x(mine), over_core(mine)
        hold = loaded[:1] if number == 0 else accs[: number - HOLD + 1][-1:] if number >= HOLD else ()
        far = over_core(tied(across, *hold) if hold else across)
        kind = jnp.float32 if start + width < channels else jnp.bfloat16
        acc = project((mine, beside, across, far), loaded, start, acc, kind)
        accs.append(acc)
        start += width
    return acc


def solution(mesh):
    in_specs = (
        P("ctx", None, "chan"),
        P(None, None, "chan"),
        P("chan", None),
        P("chan", None),
        P(None, "chan"),
    )
    return jax.shard_map(
        per_device, mesh=mesh, in_specs=in_specs, out_specs=P("ctx", "chan"), check_vma=False
    )
```

```python
import functools

import jax
import jax.numpy as jnp
from jax import lax
from jax.experimental import pallas as pl
from jax.experimental.pallas import tpu as pltpu
from jax.sharding import PartitionSpec as P

TAPS = 3
LANES = 128
ROWS = 8
INPUT_COST = 8 * 10**9
PARTS = (512, 512)
LOCAL_AT = 2
LOCAL_LIMIT = 50
INPUT_LIMIT = 52
LOAD_LIMIT = 43
LOAD_AT = (3, 4)
HOLD = 9
VMEM = pl.BlockSpec(memory_space=pltpu.VMEM)
HBM = pl.BlockSpec(memory_space=pltpu.HBM)
SMEM = pl.BlockSpec(memory_space=pltpu.SMEM)


def params(mib):
    return pltpu.CompilerParams(vmem_limit_bytes=mib * 1024 * 1024)


def cost(flops, moved):
    return pl.CostEstimate(flops=flops, bytes_accessed=moved, transcendentals=0)


def short_filter(x_ref, tokens, taps, lanes):
    out = taps[0:1, lanes] * x_ref[pl.ds(ROWS, tokens), :]
    out = out + taps[1:2, lanes] * x_ref[pl.ds(ROWS - 1, tokens), :]
    return out + taps[2:3, lanes] * x_ref[pl.ds(ROWS - 2, tokens), :]


def input_kernel(p_hbm, taps_ref, u_ref, head_ref, taps_out, kv_ref, k_pad, v_pad, sems):
    block, channels = kv_ref.shape[1:]
    cblocks = channels // LANES
    copies = [pltpu.make_async_copy(p_hbm.at[1 + i], kv_ref.at[i], sems.at[i]) for i in range(2)]
    for copy in copies:
        copy.start()
    taps_out[...] = taps_ref[...]
    k_pad[pl.ds(0, ROWS), :] = jnp.zeros((ROWS, LANES), jnp.float32)
    v_pad[pl.ds(0, ROWS), :] = jnp.zeros((ROWS, LANES), jnp.float32)
    row = lax.broadcasted_iota(jnp.int32, (ROWS, LANES), 0)
    for copy in copies:
        copy.wait()
    for c in range(cblocks):
        lanes = pl.ds(c * LANES, LANES)
        k_pad[pl.ds(ROWS, block), :] = kv_ref[0, :, lanes].astype(jnp.float32)
        v_pad[pl.ds(ROWS, block), :] = kv_ref[1, :, lanes].astype(jnp.float32)
        head_ref[0, :, lanes] = k_pad[pl.ds(ROWS, TAPS - 1), :]
        head_ref[1, :, lanes] = v_pad[pl.ds(ROWS, TAPS - 1), :]
        u = short_filter(k_pad, block, taps_ref.at[1], lanes) * short_filter(v_pad, block, taps_ref.at[2], lanes)
        for j in range(block // ROWS):
            part = u[j * ROWS : (j + 1) * ROWS]
            u_ref[pl.ds((j * cblocks + c) * ROWS, ROWS), :] = part if j else jnp.where(row < TAPS - 1, 0.0, part)


def conv_input(p, taps):
    block, channels = p.shape[1:]
    padded = pltpu.VMEM((ROWS + block, LANES), jnp.float32)
    return pl.pallas_call(
        input_kernel,
        out_shape=(
            jax.ShapeDtypeStruct((block * channels // LANES, LANES), jnp.float32),
            jax.ShapeDtypeStruct((2, TAPS - 1, channels), jnp.float32),
            jax.ShapeDtypeStruct(taps.shape, taps.dtype),
        ),
        in_specs=[HBM, VMEM],
        out_specs=(VMEM,) * 3,
        scratch_shapes=[pltpu.VMEM((2, block, channels), p.dtype), padded, padded, pltpu.SemaphoreType.DMA((2,))],
        compiler_params=params(INPUT_LIMIT),
        cost_estimate=cost(INPUT_COST, 6 * block * channels),
        name="conv_input",
    )(p, taps)


def end_state_kernel(u_ref, rates_ref, res_ref, out_ref, tables_ref):
    modes, channels = rates_ref.shape
    cblocks = channels // LANES
    groups = u_ref.shape[0] // (cblocks * ROWS)
    row = lax.broadcasted_iota(jnp.int32, (ROWS, LANES), 0).astype(jnp.float32)
    tables_ref[0] = rates_ref[...]
    tables_ref[1] = res_ref[...]

    def lane_block(c, carry):
        lanes = pl.ds(pl.multiple_of(c * LANES, LANES), LANES)
        rates = [jnp.broadcast_to(rates_ref[m : m + 1, lanes], (ROWS, LANES)) for m in range(modes)]
        steps = [jnp.exp(-float(ROWS) * r) for r in rates]
        state = [u_ref[pl.ds(pl.multiple_of(c * ROWS, ROWS), ROWS), :]] * modes
        for j in range(1, groups):
            now = u_ref[pl.ds(pl.multiple_of((j * cblocks + c) * ROWS, ROWS), ROWS), :]
            state = [a * s + now for a, s in zip(steps, state)]
        for m in range(modes):
            weighted = state[m] * jnp.exp(rates[m] * (row - (ROWS - 1.0)))
            out_ref[m : m + 1, lanes] = jnp.sum(weighted, axis=0, keepdims=True)
        return carry

    lax.fori_loop(0, cblocks, lane_block, 0)


def end_state(u, rates, residues):
    return pl.pallas_call(
        end_state_kernel,
        out_shape=(
            jax.ShapeDtypeStruct(rates.shape, jnp.float32),
            jax.ShapeDtypeStruct((2, *rates.shape), jnp.float32),
        ),
        in_specs=[VMEM] * 3,
        out_specs=(VMEM,) * 2,
        compiler_params=params(8),
        cost_estimate=cost(2 * rates.shape[0] * u.size, 4 * u.size),
        name="end_state",
    )(u, rates, residues)


def local_kernel(p_hbm, prev_ref, taps_ref, tables_ref, in_ref, first_ref, y_ref, f_ref, q_ref, x_ref, u_ref, a_ref, r_ref, q_sem):
    block, channels = q_ref.shape
    modes = tables_ref.shape[1]
    cblocks = channels // LANES
    groups = block // ROWS
    q_copy = pltpu.make_async_copy(p_hbm.at[0], q_ref, q_sem)
    q_copy.start()
    u_ref[...] = in_ref[...]
    for c in range(cblocks):
        lanes = pl.ds(c * LANES, LANES)
        for t in range(TAPS - 1):
            u_ref[pl.ds(c * ROWS + t, 1), :] = first_ref[t : t + 1, lanes]
        for m in range(0, modes, ROWS):
            rows = pl.ds(m * cblocks + c, ROWS, stride=cblocks)
            a_ref[rows, :] = jnp.exp(-tables_ref[0, m : m + ROWS, lanes])
            r_ref[rows, :] = tables_ref[1, m : m + ROWS, lanes]

    def group(j, state):
        state = list(state)
        for i in range(ROWS):
            at = pl.ds(j * ROWS * cblocks + i, cblocks, stride=ROWS)
            now = u_ref[at, :]
            total = [None] * 4
            for m in range(modes):
                a = a_ref[pl.ds(m * cblocks, cblocks), :]
                r = r_ref[pl.ds(m * cblocks, cblocks), :]
                state[m] = a * state[m] + now
                term = r * state[m]
                total[m % 4] = term if total[m % 4] is None else total[m % 4] + term
            y_ref[at, :] = (total[0] + total[1]) + (total[2] + total[3])
        return tuple(state)

    lax.fori_loop(0, groups, group, (jnp.zeros((cblocks, LANES), jnp.float32),) * modes)
    q_copy.wait()
    for c in range(cblocks):
        lanes = pl.ds(c * LANES, LANES)
        x_ref[pl.ds(ROWS - 2, 2), :] = prev_ref[0, :, lanes].astype(jnp.float32)
        x_ref[pl.ds(ROWS, block), :] = q_ref[:, lanes].astype(jnp.float32)
        feature = short_filter(x_ref, block, taps_ref.at[0], lanes)
        for j in range(groups):
            f_ref[pl.ds((j * cblocks + c) * ROWS, ROWS), :] = feature[j * ROWS : (j + 1) * ROWS]


def local_part(p, prev, taps, tables, u, first):
    block, channels = p.shape[1:]
    modes = tables.shape[1]
    cblocks = channels // LANES
    table = pltpu.VMEM((modes * cblocks, LANES), jnp.float32)
    tiled = jax.ShapeDtypeStruct((block * cblocks, LANES), jnp.float32)
    return pl.pallas_call(
        local_kernel,
        out_shape=(tiled, tiled),
        in_specs=[HBM] + [VMEM] * 5,
        out_specs=(VMEM, VMEM),
        scratch_shapes=[
            pltpu.VMEM((block, channels), p.dtype),
            pltpu.VMEM((ROWS + block, LANES), jnp.float32),
            pltpu.VMEM((block * cblocks, LANES), jnp.float32),
            table,
            table,
            pltpu.SemaphoreType.DMA,
        ],
        compiler_params=params(LOCAL_LIMIT),
        cost_estimate=cost(4 * modes * block * channels, 6 * block * channels),
        name="local_part",
    )(p, prev, taps, tables, u, first)


def gate_kernel(first, y_ref, f_ref, state_ref, tables_ref, out_ref):
    modes = tables_ref.shape[1]
    cblocks = tables_ref.shape[2] // LANES
    row = lax.broadcasted_iota(jnp.int32, (ROWS, LANES), 0).astype(jnp.float32)
    for c in range(out_ref.shape[1] // LANES):
        block = first // LANES + c
        lanes = pl.ds(first + c * LANES, LANES)
        terms, steps = [], []
        for m in range(modes):
            rate = jnp.broadcast_to(tables_ref[0, m : m + 1, lanes], (ROWS, LANES))
            scale = tables_ref[1, m : m + 1, lanes] * state_ref[m : m + 1, lanes]
            terms.append(jnp.exp(-rate * (row + 1.0)) * scale)
            steps.append(jnp.exp(-float(ROWS) * rate))

        def pair(jj, terms):
            terms = list(terms)
            both = []
            for half in range(2):
                at = pl.ds(pl.multiple_of(((2 * jj + half) * cblocks + block) * ROWS, ROWS), ROWS)
                total = [y_ref[at, :], None, None, None]
                for m in range(modes):
                    total[m % 4] = terms[m] if total[m % 4] is None else total[m % 4] + terms[m]
                    terms[m] = terms[m] * steps[m]
                both.append(f_ref[at, :] * ((total[0] + total[1]) + (total[2] + total[3])))
            rows = pl.ds(pl.multiple_of(jj * 2 * ROWS, 2 * ROWS), 2 * ROWS)
            out_ref[rows, pl.ds(c * LANES, LANES)] = jnp.concatenate(both, axis=0).astype(out_ref.dtype)
            return tuple(terms)

        lax.fori_loop(0, out_ref.shape[0] // (2 * ROWS), pair, tuple(terms), unroll=4)


def gate(first, last, y, f, state, tables):
    modes, channels = tables.shape[1:]
    block = y.shape[0] * LANES // channels
    size = block * (last - first)
    return pl.pallas_call(
        functools.partial(gate_kernel, first),
        out_shape=jax.ShapeDtypeStruct((block, last - first), jnp.bfloat16),
        in_specs=[VMEM] * 4,
        out_specs=VMEM,
        compiler_params=params(4),
        cost_estimate=cost(2 * modes * size, 6 * size),
        name="gate",
    )(y, f, state, tables)


def load_kernel(order_ref, w_hbm, *refs):
    rows_refs, sems = refs[:-1], refs[-1]
    depth = w_hbm.shape[0] // 4
    copies = []
    for number, rows_ref in enumerate(rows_refs):
        rows = pl.ds(pl.multiple_of(order_ref[number] * depth, depth), depth)
        copies.append(pltpu.make_async_copy(w_hbm.at[rows, :], rows_ref, sems.at[number]))
        copies[-1].start()
    for copy in copies:
        copy.wait()


def load_rows(order, weight):
    depth, features = weight.shape[0] // 4, weight.shape[1]
    count = order.shape[0]
    return pl.pallas_call(
        load_kernel,
        out_shape=[jax.ShapeDtypeStruct((depth, features), weight.dtype)] * count,
        in_specs=[SMEM, HBM],
        out_specs=[VMEM] * count,
        scratch_shapes=[pltpu.SemaphoreType.DMA((count,))],
        compiler_params=params(LOAD_LIMIT),
        cost_estimate=cost(0, 2 * count * depth * features),
        name="load_rows",
    )(order, weight)


def project_kernel(first, has_acc, *refs):
    count = 4
    pieces, loaded, out_ref = refs[:count], refs[count : 2 * count], refs[-1]
    total = refs[2 * count][...] if has_acc else None
    for piece, rows_ref in zip(pieces, loaded):
        rows = rows_ref[pl.ds(first, piece.shape[1]), :]
        term = jnp.dot(piece[...], rows, preferred_element_type=jnp.float32)
        total = term if total is None else total + term
    out_ref[...] = total.astype(out_ref.dtype)


def project(pieces, loaded, first, acc, kind):
    block, features = pieces[0].shape[0], loaded[0].shape[1]
    extra = [] if acc is None else [acc]
    return pl.pallas_call(
        functools.partial(project_kernel, first, len(extra)),
        out_shape=jax.ShapeDtypeStruct((block, features), kind),
        in_specs=[VMEM] * (len(pieces) + len(loaded) + len(extra)),
        out_specs=VMEM,
        compiler_params=params(8),
        cost_estimate=cost(0, 1024),
        name="project",
    )(*pieces, *loaded, *extra)


def partners(count):
    levels, size = [], 1
    while size < count:
        if size in (2, 32):
            ring = 4 if size == 2 else 8
            unit = size * 2 // ring
            flip = lambda i: (i // (unit * ring)) * unit * ring + (ring - 1 - i // unit % ring) * unit + i % unit
        else:
            flip = lambda i: i ^ size
        levels.append((size, [flip(i) for i in range(count)]))
        size *= 2
    return levels


def tied(value, *others):
    return lax.optimization_barrier((value, *others))[0]


def per_device(projected, short_taps, decay_rates, residues, out_weight):
    block, _, channels = projected.shape
    count = lax.axis_size("ctx")
    position = lax.axis_index("ctx")
    own = lax.axis_index("chan")
    order = jnp.stack([own, own ^ 1, own ^ 2, own ^ 3]).astype(jnp.int32)
    over_x = lambda value: lax.ppermute(value, "chan", [(i, i ^ 2) for i in range(4)])
    over_core = lambda value: lax.ppermute(value, "chan", [(i, i ^ 1) for i in range(4)])

    p = projected.transpose(1, 0, 2)
    prev = lax.ppermute(p[:, block - (TAPS - 1) :], "ctx", [(i, i + 1) for i in range(count - 1)])
    u, head, taps = conv_input(p, short_taps)
    total, tables = end_state(u, decay_rates.T, residues.T)
    rates = tables[0]
    head = jnp.concatenate([prev[1:].astype(jnp.float32), head], axis=1)
    feats = sum(taps[1:, j, None] * head[:, TAPS - 1 - j : 2 * (TAPS - 1) - j] for j in range(TAPS))
    first = feats[0] * feats[1]
    for t in range(TAPS - 1):
        total = total + jnp.exp(-rates * float(block - 1 - t)) * first[t][None]

    before = jnp.zeros_like(total)
    due, loaded = (), []
    levels = partners(count)
    places = [((position & size) != 0, (block * (position & (size - 1))).astype(jnp.float32)) for size, _ in levels]
    total, places, order = lax.optimization_barrier((total, places, order))
    for level, (size, partner) in enumerate(levels):
        total, before, *_ = lax.optimization_barrier((total, before, *due))
        due = ()
        other = lax.ppermute(total, "ctx", list(enumerate(partner)))
        if level == LOCAL_AT:
            y, f = local_part(p, prev, taps, tables, u, tied(first, total))
            due = (y,)
        if level in LOAD_AT:
            loaded += load_rows(tied(order, total)[len(loaded) : len(loaded) + 4 // len(LOAD_AT)], out_weight)
            due += tuple(loaded[-1:])
        later, offset = places[level]
        decay = jnp.exp(-rates * offset)
        before = before + jnp.where(later, other * decay, 0.0)
        whole = jnp.exp(-rates * float(block * size))
        total = jnp.where(later, other * whole + total, total * whole + other)

    acc, start, accs = None, 0, []
    for number, width in enumerate(PARTS):
        mine = gate(start, start + width, y, f, before, tables)
        if not loaded:
            loaded = load_rows(tied(order, mine), out_weight)
        across, beside = over_x(mine), over_core(mine)
        hold = loaded[:1] if number == 0 and not LOAD_AT else accs[: number - HOLD + 1][-1:] if number >= HOLD else ()
        far = over_core(tied(across, *hold) if hold else across)
        kind = jnp.float32 if start + width < channels else jnp.bfloat16
        acc = project((mine, beside, across, far), loaded, start, acc, kind)
        accs.append(acc)
        start += width
    return acc


def solution(mesh):
    in_specs = (
        P("ctx", None, "chan"),
        P(None, None, "chan"),
        P("chan", None),
        P("chan", None),
        P(None, "chan"),
    )
    return jax.shard_map(
        per_device, mesh=mesh, in_specs=in_specs, out_specs=P("ctx", "chan"), check_vma=False
    )
```
